32 devices in a mesh: dp: 16 (over z, x, core), mp: 2 (over y).
Axes of the slice: x: 2, y: 2, z: 4, core: 2. Of those that a mesh axis runs over, the one named last changes fastest.
Arguments:
- inputs: bfloat16 [2, 12288, 512], P(None, ('dp', 'mp')), may hold values from -6 to 6
- ff_in: bfloat16 [1, 2, 512, 2048], P(None, None, 'dp', 'mp'), may hold values from -0.25 to 0.25
- ff_out: bfloat16 [1, 2, 2048, 512], P(None, None, 'mp', 'dp'), may hold values from -0.25 to 0.25
- in_mats: bfloat16 [1, 6, 512, 512], P(None, None, 'dp', 'mp'), as said below
- attn_out: bfloat16 [1, 512, 512], P(None, 'mp', 'dp'), as said below
- conv_out: bfloat16 [1, 512, 512], P(None, 'mp', 'dp'), may hold values from -0.25 to 0.25
- dw_kernel: bfloat16 [1, 31, 512], P(None, None, ('mp', 'dp')), may hold values from -1 to 1
- bn_affine: bfloat16 [1, 2, 512], P(None, None, ('mp', 'dp')), may hold values from 0.099609375 to 1.8984375
- pos_bias: bfloat16 [1, 2, 512], P(None, None, ('mp', 'dp')), may hold values from -3 to 3
- ln_gain: float32 [1, 5, 512], P(None, None, ('dp', 'mp')), may hold values from 0.5 to 1.5
- ln_bias: float32 [1, 5, 512], P(None, None, ('dp', 'mp')), may hold values from -2 to 2
- cotangent: bfloat16 [2, 12288, 512], P(None, ('dp', 'mp')), may hold values from -6 to 6
Outputs:
- outputs: float32 [2, 12288, 512], P(None, ('dp', 'mp'))
- input_grad: float32 [2, 12288, 512], P(None, ('dp', 'mp'))
- grad_ff_in: float32 [1, 2, 512, 2048], P(None, None, 'dp', 'mp')
- grad_ff_out: float32 [1, 2, 2048, 512], P(None, None, 'mp', 'dp')
- grad_in_mats: float32 [1, 6, 512, 512], P(None, None, 'dp', 'mp')
- grad_attn_out: float32 [1, 512, 512], P(None, 'mp', 'dp')
- grad_conv_out: float32 [1, 512, 512], P(None, 'mp', 'dp')
- grad_dw_kernel: float32 [1, 31, 512], P(None, None, ('mp', 'dp'))
- grad_bn_affine: float32 [1, 2, 512], P(None, None, ('mp', 'dp'))
- grad_pos_bias: float32 [1, 2, 512], P(None, None, ('mp', 'dp'))
- grad_ln_gain: float32 [1, 5, 512], P(None, None, ('dp', 'mp'))
- grad_ln_bias: float32 [1, 5, 512], P(None, None, ('dp', 'mp'))
The draws below stay inside these ranges and needn't reach their ends.
Inputs may be any that keep to these rules, and one draw needn't show every extreme that they name: `in_mats`: mean zero, entries of order 512^(-1/2). `attn_out`: mean zero, entries of order (32 / 512)^(1/2).
All inputs are finite; a program needn't handle non-finite values.
Results may differ from the reference program's by a relative error of at most 0.034.
Values may be sent and summed in bfloat16 or wider, within the bound.
A program may use at most 256 MiB of HBM per device.

```python
import math
import jax
import jax.numpy as jnp
from jax import lax

D = 512
HEADS = 8
FF = 2048
KERNEL = 31
HEAD_DIM = 64
LENGTH = 768
MICRO = 2
LAYERS = 1
BATCH_TOK = 12288


def draw_in_mats(key, part):
    key = jax.random.fold_in(key, 11)
    shape = (LAYERS, 6, D, D)
    values = jax.random.normal(key, shape, jnp.float32) * (1.0 / math.sqrt(D))
    return values.astype(jnp.bfloat16)


def draw_attn_out(key, part):
    key = jax.random.fold_in(key, 23)
    shape = (LAYERS, D, D)
    spread_out = math.sqrt(32.0 / D)
    values = jnp.clip(jax.random.normal(key, shape, jnp.float32), -6.0, 6.0) * spread_out
    return values.astype(jnp.bfloat16)


def levels(rng, dims, split, smallest, top_value):
    level, own = 1.0, jax.random.fold_in(rng, 6)
    for axis_at, parts in split:
        heights = jnp.exp(jax.random.uniform(jax.random.fold_in(own, axis_at), (parts,), jnp.float32, smallest / len(split), top_value / len(split)))
        level = level * jnp.repeat(heights, dims[axis_at] // parts).reshape([-1 if axis == axis_at else 1 for axis in range(len(dims))])
    return level


def normal_values(rng, dims, spread, bound, shards=(), held_as=jnp.bfloat16):
    result = spread * jax.random.normal(rng, dims, jnp.float32)
    if shards:
        result = result * levels(rng, dims, shards, -0.22, 0.18)
    return jnp.clip(result, -bound, bound).astype(held_as)


def setup_inputs(seed: int = 0) -> dict:
    keys = jax.random.split(jax.random.key(seed), 13)
    inputs = normal_values(keys[0], (MICRO, BATCH_TOK, D), 1.0, 6.0, ((1, 32),))
    ff_in = normal_values(keys[1], (LAYERS, 2, D, FF), D ** -0.5, 0.25, ((2, 16), (3, 2)))
    ff_out = normal_values(keys[2], (LAYERS, 2, FF, D), (FF // 4) ** -0.5, 0.25, ((2, 2), (3, 16)))
    in_mats = draw_in_mats(jax.random.fold_in(keys[12], 71), 0)
    attn_out = draw_attn_out(jax.random.fold_in(keys[12], 71), 0)
    conv_out = normal_values(keys[5], (LAYERS, D, D), D ** -0.5, 0.25, ((1, 2), (2, 16)))
    dw_kernel = normal_values(keys[6], (LAYERS, KERNEL, D), KERNEL ** -0.5, 1.0, ((2, 32),))
    bn_affine = jnp.clip(1.0 + 0.18 * jax.random.normal(keys[7], (LAYERS, 2, D), jnp.float32), 0.099609375, 1.8984375).astype(jnp.bfloat16)
    pos_bias = normal_values(keys[8], (LAYERS, 2, D), 0.5, 3.0, ((2, 32),))
    ln_gain = jnp.clip(1.0 + 0.1 * jax.random.normal(keys[9], (LAYERS, 5, D), jnp.float32), 0.5, 1.5)
    ln_bias = normal_values(keys[10], (LAYERS, 5, D), 0.3, 2.0, ((2, 32),), jnp.float32)
    cotangent = normal_values(keys[11], (MICRO, BATCH_TOK, D), 1.0, 6.0, ((1, 32),))
    return {"inputs": inputs, "ff_in": ff_in, "ff_out": ff_out, "in_mats": in_mats, "attn_out": attn_out, "conv_out": conv_out, "dw_kernel": dw_kernel, "bn_affine": bn_affine, "pos_bias": pos_bias, "ln_gain": ln_gain, "ln_bias": ln_bias, "cotangent": cotangent}


@jax.custom_vjp
def low(v):
    return lax.optimization_barrier(v.astype(jnp.bfloat16)).astype(jnp.float32)

@jax.custom_vjp
def low_back(v):
    return v

def low_keep(v):
    return (low(v), None)

def low_pass(kept, grad):
    return (grad,)

def back_keep(v):
    return (v, None)

def back_low(kept, grad):
    return (low(grad),)
low.defvjp(low_keep, low_pass)
low_back.defvjp(back_keep, back_low)
epsilon = 1e-05
highest = lax.Precision.HIGHEST

def matmul(left, right):
    return jnp.dot(left, right, precision=highest, preferred_element_type=jnp.float32)

def relative_table(length, width):
    distance = (length - 1 - jnp.arange(2 * length - 1)).astype(jnp.float32)
    frequency = jnp.exp(jnp.arange(width // 2).astype(jnp.float32) * (-2.0 * math.log(10000.0) / width))
    angles = distance[:, None] * frequency[None, :]
    return jnp.concatenate([jnp.sin(angles), jnp.cos(angles)], axis=1)

def relative_shift(band):
    length = band.shape[-2]
    leading = band.shape[:-2]
    flattened = band.reshape(leading + (length * (2 * length - 1),))
    picked = flattened[..., length - 1:length - 1 + length * (2 * length - 2)]
    return picked.reshape(leading + (length, 2 * length - 2))[..., :length]

def layer_norm(values, gain_row, bias_row):
    center = lax.optimization_barrier(jnp.mean(values, axis=-1, keepdims=True))
    offset = values - center
    variance = lax.optimization_barrier(jnp.mean(offset * offset, axis=-1, keepdims=True))
    return offset * lax.rsqrt(variance + epsilon) * gain_row + bias_row

def feed_forward(normed, w_first, w_second):
    hidden = low(jax.nn.silu(low_back(matmul(normed, w_first))))
    return low_back(matmul(hidden, w_second))

def attention(normed, matrices, w_out, biases, sinusoid):
    score_scale = HEAD_DIM ** (-0.5)
    query_rows = low_back(matmul(normed, matrices[0]))
    key_rows = low(low_back(matmul(normed, matrices[1])))
    value_rows = low(low_back(matmul(normed, matrices[2])))
    head_shape = (-1, LENGTH, HEADS, HEAD_DIM)
    content_bias = biases[0].reshape(HEADS, HEAD_DIM)
    position_bias = biases[1].reshape(HEADS, HEAD_DIM)

    def one_sequence(pieces):
        query_seq, key_seq, value_seq = pieces
        position = low(low_back(matmul(sinusoid, matrices[3]))).reshape(2 * LENGTH - 1, HEADS, HEAD_DIM)
        with_content = low(score_scale * (query_seq + content_bias))
        with_position = low(score_scale * (query_seq + position_bias))
        content = jnp.einsum('ihd,jhd->hij', with_content, key_seq, precision=highest)
        band = jnp.einsum('ihd,rhd->hir', with_position, position, precision=highest)
        scores = low_back(content + relative_shift(band))
        row_max = lax.optimization_barrier(jnp.max(scores, axis=-1, keepdims=True))
        exponent = jnp.exp(scores - row_max)
        weights_low = low(exponent / lax.optimization_barrier(jnp.sum(exponent, axis=-1, keepdims=True)))
        context = jnp.einsum('hij,jhd->ihd', weights_low, value_seq, precision=highest)
        return context.reshape(LENGTH, HEADS * HEAD_DIM)
    context = lax.map(jax.checkpoint(one_sequence), (query_rows.reshape(head_shape), key_rows.reshape(head_shape), value_rows.reshape(head_shape)))
    context = low(low_back(context.reshape(-1, HEADS * HEAD_DIM)))
    return low_back(matmul(context, w_out))

def convolution(normed, matrices, w_out, kernel, affine):
    linear_part = low_back(matmul(normed, matrices[4]))
    gate_part = low_back(matmul(normed, matrices[5]))
    gated = (linear_part * jax.nn.sigmoid(gate_part)).reshape(-1, LENGTH, D)
    margin = (KERNEL - 1) // 2
    padded = jnp.pad(gated, ((0, 0), (margin, margin), (0, 0)))
    convolved = jnp.zeros_like(gated)
    for tap_index in range(KERNEL):
        convolved = convolved + kernel[tap_index] * padded[:, tap_index:tap_index + LENGTH, :]
    center = lax.optimization_barrier(jnp.mean(convolved, axis=(0, 1)))
    offset = convolved - center
    variance = lax.optimization_barrier(jnp.mean(offset * offset, axis=(0, 1)))
    scaled = offset * lax.rsqrt(variance + epsilon) * affine[0] + affine[1]
    active = low(jax.nn.silu(scaled))
    return low_back(matmul(active.reshape(-1, D), w_out))

def conformer_block(values, weights, layer_index, sinusoid):
    ff_in, ff_out, in_mats, attn_out, conv_out, dw_kernel, bn_affine, pos_bias, ln_gain, ln_bias = weights

    def normed_at(slot_index, source):
        return low(layer_norm(source, ln_gain[layer_index, slot_index], ln_bias[layer_index, slot_index]))
    values = values + 0.5 * feed_forward(normed_at(0, values), ff_in[layer_index, 0], ff_out[layer_index, 0])
    values = values + attention(normed_at(1, values), in_mats[layer_index], attn_out[layer_index], pos_bias[layer_index], sinusoid)
    values = values + convolution(normed_at(2, values), in_mats[layer_index], conv_out[layer_index], dw_kernel[layer_index], bn_affine[layer_index])
    values = values + 0.5 * feed_forward(normed_at(3, values), ff_in[layer_index, 1], ff_out[layer_index, 1])
    return layer_norm(values, ln_gain[layer_index, 4], ln_bias[layer_index, 4])

def reference(inputs, ff_in, ff_out, in_mats, attn_out, conv_out, dw_kernel, bn_affine, pos_bias, ln_gain, ln_bias, cotangent):
    sinusoid = low(relative_table(LENGTH, D))
    weights = tuple((array_item.astype(jnp.float32) for array_item in (ff_in, ff_out, in_mats, attn_out, conv_out, dw_kernel, bn_affine, pos_bias, ln_gain, ln_bias)))

    def forward(source, params):
        results = []
        for micro_index in range(MICRO):
            values = source[micro_index]
            for layer_index in range(LAYERS):
                values = conformer_block(values, params, layer_index, sinusoid)
            results.append(values)
        return jnp.stack(results)
    outputs, pullback = jax.vjp(forward, inputs.astype(jnp.float32), weights)
    input_grad, gradients = pullback(cotangent.astype(jnp.float32))
    return (outputs, input_grad, gradients[0], gradients[1], gradients[2], gradients[3], gradients[4], gradients[5], gradients[6], gradients[7], gradients[8], gradients[9])
```

```python
import math

import jax
import jax.numpy as jnp
from jax import lax
from jax.sharding import PartitionSpec as P

D = 512
HEADS = 8
HEAD_DIM = 64
FF = 2048
KERNEL = 31
LENGTH = 768
LANES = 128

epsilon = 1e-05
bfloat = jnp.bfloat16
single = jnp.float32
EVERY = ("mp", "dp")


def dot(spec, left, right):
    return jnp.einsum(spec, left, right, preferred_element_type=single)


def sinusoids(length, width):
    frequency = jnp.exp(
        jnp.arange(width // 2).astype(single) * (-2.0 * math.log(10000.0) / width)
    )
    angles = jnp.arange(length).astype(single)[:, None] * frequency[None, :]
    return (jnp.sin(angles), jnp.cos(angles))


def norm_rows(values, gain_row, bias_row):
    center = jnp.mean(values, axis=-1, keepdims=True)
    offset = values - center
    inverse_std = lax.rsqrt(jnp.mean(offset * offset, axis=-1, keepdims=True) + epsilon)
    unit_rows = offset * inverse_std
    return (unit_rows * gain_row + bias_row, (unit_rows, inverse_std))


def norm_rows_back(grad_normed, kept, gain_row):
    unit_rows, inverse_std = kept
    grad_unit = grad_normed * gain_row
    grad_values = inverse_std * (
        grad_unit
        - jnp.mean(grad_unit, axis=-1, keepdims=True)
        - unit_rows * jnp.mean(grad_unit * unit_rows, axis=-1, keepdims=True)
    )
    return (grad_values, jnp.sum(grad_normed * unit_rows, axis=0), jnp.sum(grad_normed, axis=0))


def swish_slope(values):
    sigmoid = jax.nn.sigmoid(values)
    return sigmoid * (1.0 + values * (1.0 - sigmoid))


def depthwise(gated, taps):
    kernel_size = taps.shape[0]
    margin = (kernel_size - 1) // 2
    length = gated.shape[1]
    padded = jnp.pad(gated, ((0, 0), (margin, margin), (0, 0)))
    convolved = jnp.zeros_like(gated)
    for tap_index in range(kernel_size):
        convolved = convolved + taps[tap_index] * padded[:, tap_index : tap_index + length, :]
    return convolved


def depthwise_back(gated, grad_convolved, taps):
    kernel_size = taps.shape[0]
    margin = (kernel_size - 1) // 2
    length = gated.shape[1]
    padded = jnp.pad(gated, ((0, 0), (margin, margin), (0, 0)))
    grad_padded = jnp.pad(grad_convolved, ((0, 0), (margin, margin), (0, 0)))
    grad_gated = jnp.zeros_like(gated)
    grad_taps = []
    for tap_index in range(kernel_size):
        begin = 2 * margin - tap_index
        grad_gated = grad_gated + taps[tap_index] * grad_padded[:, begin : begin + length, :]
        grad_taps.append(
            jnp.sum(padded[:, tap_index : tap_index + length, :] * grad_convolved, axis=(0, 1))
        )
    return (grad_gated, jnp.stack(grad_taps))


def per_device(
    inputs,
    ff_in,
    ff_out,
    in_mats,
    attn_out,
    conv_out,
    dw_kernel,
    bn_affine,
    pos_bias,
    ln_gain,
    ln_bias,
    cotangent,
):
    mp = lax.axis_size("mp")
    dp = lax.axis_size("dp")
    owners = mp * dp
    micro = inputs.shape[0]
    local_rows = inputs.shape[1]
    group_rows = local_rows * mp
    sequences = group_rows // LENGTH
    total_rows = group_rows * dp
    own = D // owners
    depth = D // dp
    score_scale = HEAD_DIM ** (-0.5)
    me = lax.axis_index("mp")
    mine = me % micro
    swap = [(0, 1), (1, 0)]
    paired = mp == 2 and micro == 2

    def enter(blocks):
        if paired:
            other = lax.ppermute(jnp.where(me == 0, blocks[1], blocks[0]), "mp", swap)
            first = jnp.where(me == 0, blocks[0], other)
            second = jnp.where(me == 0, other, blocks[1])
            return jnp.concatenate([first, second], axis=0)
        whole = lax.all_gather(blocks, "mp", axis=1, tiled=True)
        return lax.dynamic_index_in_dim(whole, mine, axis=0, keepdims=False)

    def leave(rows):
        if paired:
            upper, lower = rows[:local_rows], rows[local_rows:]
            sent = jnp.where(me == 0, lower, upper).astype(bfloat)
            other = lax.ppermute(sent, "mp", swap).astype(single)
            return jnp.stack(
                [jnp.where(me == 0, upper, other), jnp.where(me == 0, other, lower)]
            )
        whole = lax.all_gather(rows.astype(bfloat), "mp", axis=0)[:micro]
        return lax.dynamic_slice_in_dim(whole, me * local_rows, local_rows, axis=1).astype(single)

    pair_in = ff_in[0]
    pair_out = jnp.swapaxes(ff_out[0], 1, 2)
    gain_high = lax.reduce_precision(ln_gain[0], 8, 7)
    bias_high = lax.reduce_precision(ln_bias[0], 8, 7)
    small = jnp.concatenate(
        [
            dw_kernel[0],
            bn_affine[0],
            pos_bias[0],
            gain_high.astype(bfloat),
            bias_high.astype(bfloat),
            (ln_gain[0] - gain_high).astype(bfloat),
            (ln_bias[0] - bias_high).astype(bfloat),
        ],
        axis=0,
    )
    small_rows = small.shape[0]

    def fold(flat):
        spacing = [(0, 0)] * (flat.ndim - 1) + [(0, depth * LANES - flat.shape[-1])]
        return jnp.pad(flat, spacing).reshape(flat.shape[:-1] + (depth, LANES))

    def gather(parts):
        block = jnp.concatenate(parts, axis=1)
        return lax.all_gather(block, EVERY, axis=0, tiled=True).reshape(mp, D, -1)

    def unpack(packed, first, width):
        part = packed[:, :, first : first + width]
        return jnp.swapaxes(part, 0, 1).reshape(D, mp * width)

    hidden_width = FF // mp
    width = D // mp
    packed = gather([pair_in[0], pair_out[0], fold(small.reshape(-1))])
    in_zero = unpack(packed, 0, hidden_width)
    out_zero = unpack(packed, hidden_width, hidden_width)
    small_all = (
        packed[:, :, 2 * hidden_width :]
        .reshape(owners, depth * LANES)[:, : small_rows * own]
        .reshape(owners, small_rows, own)
    )
    channel_rows = KERNEL + 4
    channel = jnp.swapaxes(small_all[:, :channel_rows], 0, 1).reshape(channel_rows, D)
    channel = channel.astype(single)
    norm_rows_all = (
        small_all[:, channel_rows:]
        .reshape(mp, dp, 4, 5, own)
        .transpose(2, 3, 1, 0, 4)
        .reshape(4, 5, D)
        .astype(single)
    )
    norm_gain = norm_rows_all[0] + norm_rows_all[2]
    norm_bias = norm_rows_all[1] + norm_rows_all[3]
    taps, affine, biases = channel[:KERNEL], channel[KERNEL : KERNEL + 2], channel[KERNEL + 2 :]

    packed = gather(
        [in_mats[0, k] for k in range(6)] + [attn_out[0].T, conv_out[0].T]
    )
    mats = [unpack(packed, k * width, width) for k in range(8)]
    w_position, w_attn, w_conv = (mats[3], mats[6], mats[7])
    w_query = jnp.concatenate(mats[0:3], axis=1)
    w_gate = jnp.concatenate(mats[4:6], axis=1)
    packed = gather([pair_in[1], pair_out[1]])
    in_one = unpack(packed, 0, hidden_width)
    out_one = unpack(packed, hidden_width, hidden_width)

    def norm_input(values, slot):
        normed, kept = norm_rows(values, norm_gain[slot], norm_bias[slot])
        return (normed.astype(bfloat), kept)

    def ff_forward(rows, w_first, w_second):
        hidden_pre = dot("gd,df->gf", rows, w_first)
        hidden = jax.nn.silu(hidden_pre).astype(bfloat)
        return (dot("gf,df->gd", hidden, w_second), (hidden_pre, hidden))

    def ff_backward(grad_out, rows, kept, w_first, w_second):
        hidden_pre, hidden = kept
        grad_second = dot("gd,gf->df", grad_out, hidden)
        grad_hidden = dot("gd,df->gf", grad_out, w_second)
        grad_pre = (grad_hidden * swish_slope(hidden_pre)).astype(bfloat)
        grad_first = dot("gd,gf->df", rows, grad_pre)
        return (dot("gf,df->gd", grad_pre, w_first), grad_first, grad_second)

    sine, cosine = sinusoids(LENGTH, D)
    angle_rows = jnp.concatenate([cosine, sine], axis=1).astype(bfloat)
    position_heads = w_position.reshape(D, HEADS, HEAD_DIM)

    def by_head(values):
        return values.reshape(sequences, LENGTH, HEADS, HEAD_DIM).transpose(0, 2, 1, 3)

    def by_row(values):
        return values.transpose(0, 2, 1, 3).reshape(group_rows, D)

    def attention_forward(rows):
        projected = dot("gd,dc->gc", rows, w_query)
        query_rows = projected[:, :D]
        key_rows = by_head(projected[:, D : 2 * D].astype(bfloat))
        value_rows = by_head(projected[:, 2 * D :].astype(bfloat))
        with_content = by_head((score_scale * (query_rows + biases[0])).astype(bfloat))
        with_position = by_head((score_scale * (query_rows + biases[1])).astype(bfloat))
        turned = dot("shid,khd->shik", with_position, position_heads)
        on_sine, on_cosine = turned[..., : D // 2], turned[..., D // 2 :]
        turned = jnp.concatenate(
            [on_sine * sine + on_cosine * cosine, on_cosine * sine - on_sine * cosine], axis=-1
        ).astype(bfloat)
        scores = dot("shid,shjd->shij", with_content, key_rows) + dot(
            "shik,jk->shij", turned, angle_rows
        )
        row_max = jnp.max(scores, axis=-1, keepdims=True)
        exponent = jnp.exp(scores - row_max)
        row_total = jnp.sum(exponent, axis=-1, keepdims=True)
        probs = (exponent / row_total).astype(bfloat)
        context = dot("shij,shjd->shid", probs, value_rows)
        context_rows = by_row(context.astype(bfloat))
        branch = dot("gc,dc->gd", context_rows, w_attn)
        return (
            branch,
            (with_content, with_position, key_rows, value_rows, probs, context, context_rows),
        )

    def attention_backward(grad_out, rows, kept):
        with_content, with_position, key_rows, value_rows, probs, context, context_rows = kept
        grad_attn = dot("gd,gc->dc", grad_out, context_rows)
        grad_context = by_head(dot("gd,dc->gc", grad_out, w_attn).astype(bfloat))
        grad_probs = dot("shid,shjd->shij", grad_context, value_rows)
        grad_value = dot("shij,shid->shjd", probs, grad_context)
        shared = jnp.sum(grad_context.astype(single) * context, axis=-1, keepdims=True)
        grad_scores = (probs.astype(single) * (grad_probs - shared)).astype(bfloat)
        grad_content = dot("shij,shjd->shid", grad_scores, key_rows)
        grad_key = dot("shij,shid->shjd", grad_scores, with_content)
        grad_turned = dot("shij,jk->shik", grad_scores, angle_rows)
        on_first, on_second = grad_turned[..., : D // 2], grad_turned[..., D // 2 :]
        grad_turned = jnp.concatenate(
            [on_first * sine - on_second * cosine, on_first * cosine + on_second * sine], axis=-1
        ).astype(bfloat)
        grad_posq = dot("shik,khd->shid", grad_turned, position_heads)
        grad_position = dot("shik,shid->khd", grad_turned, with_position).reshape(D, D)
        grad_bias = score_scale * jnp.stack(
            [
                jnp.sum(grad_content, axis=(0, 2)).reshape(D),
                jnp.sum(grad_posq, axis=(0, 2)).reshape(D),
            ]
        )
        stacked = jnp.concatenate(
            [
                by_row((score_scale * (grad_content + grad_posq)).astype(bfloat)),
                by_row(grad_key.astype(bfloat)),
                by_row(grad_value.astype(bfloat)),
            ],
            axis=1,
        )
        grad_query = dot("gd,gc->dc", rows, stacked)
        grad_rows = dot("gc,dc->gd", stacked, w_query)
        return (grad_rows, grad_query, grad_position, grad_attn, grad_bias)

    values = enter(inputs).astype(single)
    cotangent_rows = enter(cotangent).astype(single)
    rows_one, norm_one = norm_input(values, 0)
    branch, ff_first = ff_forward(rows_one, in_zero, out_zero)
    after_one = values + 0.5 * branch
    rows_two, norm_two = norm_input(after_one, 1)
    branch, attn_kept = attention_forward(rows_two)
    after_two = after_one + branch
    rows_three, norm_three = norm_input(after_two, 2)
    projected = dot("gd,dc->gc", rows_three, w_gate)
    linear_part, gate_part = projected[:, :D], projected[:, D:]
    gated = (linear_part * jax.nn.sigmoid(gate_part)).reshape(sequences, LENGTH, D)
    convolved = depthwise(gated, taps).reshape(group_rows, D)
    local_center = jnp.mean(convolved, axis=0)
    local_offset = convolved - local_center
    moments = lax.all_gather(
        jnp.stack([local_center, jnp.sum(local_offset * local_offset, axis=0)]), "dp", axis=0
    )
    center = jnp.mean(moments[:, 0], axis=0)
    spread = moments[:, 0] - center
    variance = (jnp.sum(moments[:, 1], axis=0) + group_rows * jnp.sum(spread * spread, axis=0)) / (
        total_rows
    )
    inverse_std = lax.rsqrt(variance + epsilon)
    unit_values = (convolved - center) * inverse_std
    scaled = unit_values * affine[0] + affine[1]
    active = jax.nn.silu(scaled).astype(bfloat)
    after_three = after_two + dot("gc,dc->gd", active, w_conv)
    rows_four, norm_four = norm_input(after_three, 3)
    branch, ff_second = ff_forward(rows_four, in_one, out_one)
    after_four = after_three + 0.5 * branch
    result, norm_five = norm_rows(after_four, norm_gain[4], norm_bias[4])
    outputs = leave(result)

    counts = (me < micro).astype(single)

    def scatter(parts):
        blocks = [
            jnp.swapaxes(part.astype(bfloat).reshape(D, mp, -1), 0, 1) for part in parts[0]
        ] + parts[1]
        block = jnp.concatenate(blocks, axis=2)
        if mp != micro:
            block = block * counts.astype(bfloat)
        return lax.psum_scatter(
            block.reshape(mp * D, -1), EVERY, scatter_dimension=0, tiled=True
        ).astype(single)

    gains = [None] * 5
    shifts = [None] * 5
    grad_four, gains[4], shifts[4] = norm_rows_back(cotangent_rows, norm_five, norm_gain[4])
    grad_rows, first_one, second_one = ff_backward(
        (0.5 * grad_four).astype(bfloat), rows_four, ff_second, in_one, out_one
    )
    owned_one = scatter(([first_one, second_one], []))
    grad_norm, gains[3], shifts[3] = norm_rows_back(grad_rows, norm_four, norm_gain[3])
    grad_three = grad_four + grad_norm
    grad_out = grad_three.astype(bfloat)
    grad_conv = dot("gd,gc->dc", grad_out, active)
    grad_scaled = dot("gd,dc->gc", grad_out, w_conv) * swish_slope(scaled)
    local_shift = jnp.sum(grad_scaled, axis=0)
    local_scale = jnp.sum(grad_scaled * unit_values, axis=0)
    sums = jnp.sum(lax.all_gather(jnp.stack([local_shift, local_scale]), "dp", axis=0), axis=0)
    grad_convolved = (
        affine[0]
        * inverse_std
        * (grad_scaled - sums[0] / total_rows - unit_values * (sums[1] / total_rows))
    )
    grad_gated, grad_taps = depthwise_back(
        gated, grad_convolved.reshape(sequences, LENGTH, D), taps
    )
    grad_gated = grad_gated.reshape(group_rows, D)
    sigmoid = jax.nn.sigmoid(gate_part)
    stacked = jnp.concatenate(
        [
            (grad_gated * sigmoid).astype(bfloat),
            (grad_gated * linear_part * sigmoid * (1.0 - sigmoid)).astype(bfloat),
        ],
        axis=1,
    )
    grad_gate = dot("gd,gc->dc", rows_three, stacked)
    grad_rows = dot("gc,dc->gd", stacked, w_gate)
    grad_norm, gains[2], shifts[2] = norm_rows_back(grad_rows, norm_three, norm_gain[2])
    grad_two = grad_three + grad_norm
    grad_rows, grad_query, grad_position, grad_attn, grad_bias = attention_backward(
        grad_two.astype(bfloat), rows_two, attn_kept
    )
    owned_mats = scatter(
        (
            [grad_query[:, k * D : (k + 1) * D] for k in range(3)]
            + [grad_position, grad_gate[:, :D], grad_gate[:, D:], grad_attn, grad_conv],
            [],
        )
    )
    grad_norm, gains[1], shifts[1] = norm_rows_back(grad_rows, norm_two, norm_gain[1])
    grad_one = grad_two + grad_norm
    grad_rows, first_zero, second_zero = ff_backward(
        (0.5 * grad_one).astype(bfloat), rows_one, ff_first, in_zero, out_zero
    )
    grad_norm, gains[0], shifts[0] = norm_rows_back(grad_rows, norm_one, norm_gain[0])
    input_grad = leave(grad_one + grad_norm)
    channel_grads = jnp.concatenate(
        [grad_taps, jnp.stack([local_scale, local_shift]), grad_bias], axis=0
    )
    channel_grads = jnp.swapaxes(channel_grads.reshape(channel_rows, owners, own), 0, 1)
    norm_grads = (
        jnp.stack(gains + shifts).reshape(10, dp, mp, own).transpose(2, 1, 0, 3)
    ).reshape(owners, 10, own)
    small_grads = jnp.concatenate([channel_grads, norm_grads], axis=1).reshape(owners, -1)
    owned_zero = scatter(
        ([first_zero, second_zero], [fold(small_grads.astype(bfloat)).reshape(mp, D, LANES)])
    )
    owned_small = owned_zero[:, 2 * hidden_width :].reshape(-1)[: (channel_rows + 10) * own]
    owned_small = owned_small.reshape(1, channel_rows + 10, own)

    def halves(owned):
        return (owned[:, :hidden_width], owned[:, hidden_width : 2 * hidden_width].T)

    first_zero, second_zero = halves(owned_zero)
    first_one, second_one = halves(owned_one)
    owned_list = [owned_mats[:, k * width : (k + 1) * width] for k in range(8)]
    return (
        outputs,
        input_grad,
        jnp.stack([first_zero, first_one])[None],
        jnp.stack([second_zero, second_one])[None],
        jnp.stack(owned_list[:6])[None],
        owned_list[6].T[None],
        owned_list[7].T[None],
        owned_small[:, :KERNEL],
        owned_small[:, KERNEL : KERNEL + 2],
        owned_small[:, KERNEL + 2 : channel_rows],
        owned_small[:, channel_rows : channel_rows + 5],
        owned_small[:, channel_rows + 5 :],
    )


def solution(mesh):
    placed = (
        P(None, ("dp", "mp"), None),
        P(None, None, "dp", "mp"),
        P(None, None, "mp", "dp"),
        P(None, None, "dp", "mp"),
        P(None, "mp", "dp"),
        P(None, "mp", "dp"),
        P(None, None, ("mp", "dp")),
        P(None, None, ("mp", "dp")),
        P(None, None, ("mp", "dp")),
        P(None, None, ("dp", "mp")),
        P(None, None, ("dp", "mp")),
        P(None, ("dp", "mp"), None),
    )
    return jax.shard_map(
        per_device,
        mesh=mesh,
        in_specs=placed,
        out_specs=(
            P(None, ("dp", "mp"), None),
            P(None, ("dp", "mp"), None),
            P(None, None, "dp", "mp"),
            P(None, None, "mp", "dp"),
            P(None, None, "dp", "mp"),
            P(None, "mp", "dp"),
            P(None, "mp", "dp"),
            P(None, None, ("mp", "dp")),
            P(None, None, ("mp", "dp")),
            P(None, None, ("mp", "dp")),
            P(None, None, ("dp", "mp")),
            P(None, None, ("dp", "mp")),
        ),
        check_vma=False,
    )
```

```python
import math

import jax
import jax.numpy as jnp
from jax import lax
from jax.sharding import PartitionSpec as P

D = 512
HEADS = 8
HEAD_DIM = 64
FF = 2048
KERNEL = 31
LENGTH = 768
LANES = 128

epsilon = 1e-05
bfloat = jnp.bfloat16
single = jnp.float32
EVERY = ("mp", "dp")


def dot(spec, left, right):
    return jnp.einsum(spec, left, right, preferred_element_type=single)


def sinusoids(length, width):
    frequency = jnp.exp(
        jnp.arange(width // 2).astype(single) * (-2.0 * math.log(10000.0) / width)
    )
    angles = jnp.arange(length).astype(single)[:, None] * frequency[None, :]
    return (jnp.sin(angles), jnp.cos(angles))


def norm_rows(values, gain_row, bias_row):
    center = jnp.mean(values, axis=-1, keepdims=True)
    offset = values - center
    inverse_std = lax.rsqrt(jnp.mean(offset * offset, axis=-1, keepdims=True) + epsilon)
    unit_rows = offset * inverse_std
    return (unit_rows * gain_row + bias_row, (unit_rows, inverse_std))


def norm_rows_back(grad_normed, kept, gain_row):
    unit_rows, inverse_std = kept
    grad_unit = grad_normed * gain_row
    grad_values = inverse_std * (
        grad_unit
        - jnp.mean(grad_unit, axis=-1, keepdims=True)
        - unit_rows * jnp.mean(grad_unit * unit_rows, axis=-1, keepdims=True)
    )
    return (grad_values, jnp.sum(grad_normed * unit_rows, axis=0), jnp.sum(grad_normed, axis=0))


def swish_slope(values):
    sigmoid = jax.nn.sigmoid(values)
    return sigmoid * (1.0 + values * (1.0 - sigmoid))


def stack_rows(rows):
    place = lax.broadcasted_iota(jnp.int32, (len(rows), rows[0].shape[0]), 0)
    stacked = jnp.zeros(place.shape, single)
    for index, row in enumerate(rows):
        stacked = jnp.where(place == index, row[None, :], stacked)
    return stacked


def depthwise(gated, taps):
    kernel_size = taps.shape[0]
    margin = (kernel_size - 1) // 2
    length = gated.shape[1]
    padded = jnp.pad(gated, ((0, 0), (margin, margin), (0, 0)))
    convolved = jnp.zeros_like(gated)
    for tap_index in range(kernel_size):
        convolved = convolved + taps[tap_index] * padded[:, tap_index : tap_index + length, :]
    return convolved


def depthwise_back(gated, grad_convolved, taps):
    kernel_size = taps.shape[0]
    margin = (kernel_size - 1) // 2
    length = gated.shape[1]
    padded = jnp.pad(gated, ((0, 0), (margin, margin), (0, 0)))
    grad_padded = jnp.pad(grad_convolved, ((0, 0), (margin, margin), (0, 0)))
    grad_gated = jnp.zeros_like(gated)
    grad_taps = []
    for tap_index in range(kernel_size):
        begin = 2 * margin - tap_index
        grad_gated = grad_gated + taps[tap_index] * grad_padded[:, begin : begin + length, :]
        grad_taps.append(
            jnp.sum(padded[:, tap_index : tap_index + length, :] * grad_convolved, axis=(0, 1))
        )
    return (grad_gated, stack_rows(grad_taps))


def per_device(
    inputs,
    ff_in,
    ff_out,
    in_mats,
    attn_out,
    conv_out,
    dw_kernel,
    bn_affine,
    pos_bias,
    ln_gain,
    ln_bias,
    cotangent,
):
    mp = lax.axis_size("mp")
    dp = lax.axis_size("dp")
    owners = mp * dp
    micro = inputs.shape[0]
    local_rows = inputs.shape[1]
    group_rows = local_rows * mp
    sequences = group_rows // LENGTH
    total_rows = group_rows * dp
    own = D // owners
    depth = D // dp
    score_scale = HEAD_DIM ** (-0.5)
    me = lax.axis_index("mp")
    mine = me % micro
    swap = [(0, 1), (1, 0)]
    paired = mp == 2 and micro == 2

    def enter(blocks):
        if paired:
            other = lax.ppermute(jnp.where(me == 0, blocks[1], blocks[0]), "mp", swap)
            first = jnp.where(me == 0, blocks[0], other)
            second = jnp.where(me == 0, other, blocks[1])
            return jnp.concatenate([first, second], axis=0)
        whole = lax.all_gather(blocks, "mp", axis=1, tiled=True)
        return lax.dynamic_index_in_dim(whole, mine, axis=0, keepdims=False)

    def leave(rows):
        if paired:
            upper, lower = rows[:local_rows], rows[local_rows:]
            sent = jnp.where(me == 0, lower, upper).astype(bfloat)
            other = lax.ppermute(sent, "mp", swap).astype(single)
            return jnp.stack(
                [jnp.where(me == 0, upper, other), jnp.where(me == 0, other, lower)]
            )
        whole = lax.all_gather(rows.astype(bfloat), "mp", axis=0)[:micro]
        return lax.dynamic_slice_in_dim(whole, me * local_rows, local_rows, axis=1).astype(single)

    pair_in = ff_in[0]
    pair_out = jnp.swapaxes(ff_out[0], 1, 2)
    gain_high = lax.reduce_precision(ln_gain[0], 8, 7)
    bias_high = lax.reduce_precision(ln_bias[0], 8, 7)
    small = jnp.concatenate(
        [
            dw_kernel[0],
            bn_affine[0],
            pos_bias[0],
            gain_high.astype(bfloat),
            bias_high.astype(bfloat),
            (ln_gain[0] - gain_high).astype(bfloat),
            (ln_bias[0] - bias_high).astype(bfloat),
        ],
        axis=0,
    )
    small_rows = small.shape[0]

    def fold(flat):
        spacing = [(0, 0)] * (flat.ndim - 1) + [(0, depth * LANES - flat.shape[-1])]
        return jnp.pad(flat, spacing).reshape(flat.shape[:-1] + (depth, LANES))

    def gather(block):
        return lax.all_gather(block, EVERY, axis=0, tiled=True).reshape(mp, D, -1)

    dp_bits = list(range(dp.bit_length() - 1))
    mp_bits = list(range(mp.bit_length() - 1))
    exchanges = (
        [("dp", bit) for bit in dp_bits[:2]]
        + [("mp", bit) for bit in mp_bits]
        + [("dp", bit) for bit in dp_bits[2:]]
    )
    sizes = {"dp": dp, "mp": mp}

    def partner(values, axis, bit):
        return lax.ppermute(values, axis, [(i, i ^ (1 << bit)) for i in range(sizes[axis])])

    def own_bit(axis, bit):
        return (lax.axis_index(axis) >> bit) & 1

    def gather_by_pairs(block):
        held = block[None, None]
        for axis, bit in reversed(exchanges):
            other = partner(held, axis, bit)
            low = own_bit(axis, bit) == 0
            where = 1 if axis == "mp" else 2
            pair = [jnp.where(low, held, other), jnp.where(low, other, held)]
            shape = list(held.shape)
            shape[where - 1] *= 2
            held = jnp.stack(pair, axis=where).reshape(shape)
        return held.reshape(mp, D, -1)

    def sum_by_pairs(blocks):
        held = blocks.reshape(mp, dp, depth, -1)
        for axis, bit in exchanges:
            shape = list(held.shape)
            where = 0 if axis == "mp" else 1
            shape[where : where + 1] = [shape[where] // 2, 2]
            split = held.reshape(shape)
            choice = own_bit(axis, bit)
            sent = lax.dynamic_index_in_dim(split, 1 - choice, axis=where + 1, keepdims=False)
            kept = lax.dynamic_index_in_dim(split, choice, axis=where + 1, keepdims=False)
            other = partner(sent, axis, bit)
            held = (kept.astype(single) + other.astype(single)).astype(bfloat)
        return held.reshape(depth, -1)

    def unpack(packed, first, width):
        part = packed[:, :, first : first + width]
        return jnp.swapaxes(part, 0, 1).reshape(D, mp * width)

    hidden_width = FF // mp
    width = D // mp
    packed = gather(
        jnp.concatenate([pair_in[0], pair_out[0], fold(small.reshape(-1))], axis=1)
    )
    packed_zero = packed
    in_zero = packed[:, :, :hidden_width]
    out_zero = packed[:, :, hidden_width : 2 * hidden_width]
    small_all = (
        packed[:, :, 2 * hidden_width :]
        .reshape(owners, depth * LANES)[:, : small_rows * own]
        .reshape(owners, small_rows, own)
    )
    channel_rows = KERNEL + 4
    channel = jnp.swapaxes(small_all[:, :channel_rows], 0, 1).reshape(channel_rows, D)
    channel = channel.astype(single)
    norm_rows_all = (
        small_all[:, channel_rows:]
        .reshape(mp, dp, 4, 5, own)
        .transpose(2, 3, 1, 0, 4)
        .reshape(4, 5, D)
        .astype(single)
    )
    norm_gain = norm_rows_all[0] + norm_rows_all[2]
    norm_bias = norm_rows_all[1] + norm_rows_all[3]
    taps, affine, biases = channel[:KERNEL], channel[KERNEL : KERNEL + 2], channel[KERNEL + 2 :]

    packed = gather_by_pairs(
        jnp.concatenate(
            [in_mats[0, k] for k in range(6)] + [attn_out[0].T, conv_out[0].T], axis=1
        )
    )
    mats = [unpack(packed, k * width, width) for k in range(8)]
    w_position, w_attn, w_conv = (mats[3], mats[6], mats[7])
    w_query = jnp.concatenate(mats[0:3], axis=1)
    w_gate = jnp.concatenate(mats[4:6], axis=1)
    block_one = jnp.concatenate([pair_in[1], pair_out[1]], axis=1)
    block_one, _ = lax.optimization_barrier((block_one, packed_zero))
    packed = gather(block_one)
    in_one = packed[:, :, :hidden_width]
    out_one = packed[:, :, hidden_width:]

    def norm_input(values, slot):
        normed, kept = norm_rows(values, norm_gain[slot], norm_bias[slot])
        return (normed.astype(bfloat), kept)

    def ff_forward(rows, w_first, w_second):
        hidden_pre = dot("gd,mdf->mgf", rows, w_first)
        hidden = jax.nn.silu(hidden_pre).astype(bfloat)
        return (dot("mgf,mdf->gd", hidden, w_second), (hidden_pre, hidden))

    def ff_backward(grad_out, rows, kept, w_first, w_second):
        hidden_pre, hidden = kept
        grad_second = dot("gd,mgf->mdf", grad_out, hidden)
        grad_hidden = dot("gd,mdf->mgf", grad_out, w_second)
        grad_pre = (grad_hidden * swish_slope(hidden_pre)).astype(bfloat)
        grad_first = dot("gd,mgf->mdf", rows, grad_pre)
        return (dot("mgf,mdf->gd", grad_pre, w_first), grad_first, grad_second)

    sine, cosine = sinusoids(LENGTH, D)
    angle_rows = jnp.concatenate([cosine, sine], axis=1).astype(bfloat)
    position_heads = w_position.reshape(D, HEADS, HEAD_DIM)

    def by_head(values):
        return values.reshape(sequences, LENGTH, HEADS, HEAD_DIM).transpose(0, 2, 1, 3)

    def by_row(values):
        return values.transpose(0, 2, 1, 3).reshape(group_rows, D)

    def attention_forward(rows):
        projected = dot("gd,dc->gc", rows, w_query)
        query_rows = projected[:, :D]
        key_rows = by_head(projected[:, D : 2 * D].astype(bfloat))
        value_rows = by_head(projected[:, 2 * D :].astype(bfloat))
        with_content = by_head((score_scale * (query_rows + biases[0])).astype(bfloat))
        with_position = by_head((score_scale * (query_rows + biases[1])).astype(bfloat))
        turned = dot("shid,khd->shik", with_position, position_heads)
        on_sine, on_cosine = turned[..., : D // 2], turned[..., D // 2 :]
        turned = jnp.concatenate(
            [on_sine * sine + on_cosine * cosine, on_cosine * sine - on_sine * cosine], axis=-1
        ).astype(bfloat)
        scores = dot("shid,shjd->shij", with_content, key_rows) + dot(
            "shik,jk->shij", turned, angle_rows
        )
        row_max = jnp.max(scores, axis=-1, keepdims=True)
        exponent = jnp.exp(scores - row_max)
        row_total = jnp.sum(exponent, axis=-1, keepdims=True)
        probs = (exponent / row_total).astype(bfloat)
        context = dot("shij,shjd->shid", probs, value_rows)
        context_rows = by_row(context.astype(bfloat))
        branch = dot("gc,dc->gd", context_rows, w_attn)
        return (
            branch,
            (with_content, with_position, key_rows, value_rows, probs, context, context_rows),
        )

    def attention_backward(grad_out, rows, kept):
        with_content, with_position, key_rows, value_rows, probs, context, context_rows = kept
        grad_attn = dot("gd,gc->dc", grad_out, context_rows)
        grad_context = by_head(dot("gd,dc->gc", grad_out, w_attn).astype(bfloat))
        grad_probs = dot("shid,shjd->shij", grad_context, value_rows)
        grad_value = dot("shij,shid->shjd", probs, grad_context)
        shared = jnp.sum(grad_context.astype(single) * context, axis=-1, keepdims=True)
        grad_scores = (probs.astype(single) * (grad_probs - shared)).astype(bfloat)
        grad_content = dot("shij,shjd->shid", grad_scores, key_rows)
        grad_key = dot("shij,shid->shjd", grad_scores, with_content)
        grad_turned = dot("shij,jk->shik", grad_scores, angle_rows)
        on_first, on_second = grad_turned[..., : D // 2], grad_turned[..., D // 2 :]
        grad_turned = jnp.concatenate(
            [on_first * sine - on_second * cosine, on_first * cosine + on_second * sine], axis=-1
        ).astype(bfloat)
        grad_posq = dot("shik,khd->shid", grad_turned, position_heads)
        grad_position = dot("shik,shid->khd", grad_turned, with_position).reshape(D, D)
        grad_bias = score_scale * jnp.stack(
            [
                jnp.sum(grad_content, axis=(0, 2)).reshape(D),
                jnp.sum(grad_posq, axis=(0, 2)).reshape(D),
            ]
        )
        stacked = jnp.concatenate(
            [
                by_row((score_scale * (grad_content + grad_posq)).astype(bfloat)),
                by_row(grad_key.astype(bfloat)),
                by_row(grad_value.astype(bfloat)),
            ],
            axis=1,
        )
        grad_query = dot("gd,gc->dc", rows, stacked)
        grad_rows = dot("gc,dc->gd", stacked, w_query)
        return (grad_rows, grad_query, grad_position, grad_attn, grad_bias)

    values = enter(inputs).astype(single)
    cotangent_rows = enter(cotangent).astype(single)
    rows_one, norm_one = norm_input(values, 0)
    branch, ff_first = ff_forward(rows_one, in_zero, out_zero)
    after_one = values + 0.5 * branch
    rows_two, norm_two = norm_input(after_one, 1)
    branch, attn_kept = attention_forward(rows_two)
    after_two = after_one + branch
    rows_three, norm_three = norm_input(after_two, 2)
    projected = dot("gd,dc->gc", rows_three, w_gate)
    linear_part, gate_part = projected[:, :D], projected[:, D:]
    gated = (linear_part * jax.nn.sigmoid(gate_part)).reshape(sequences, LENGTH, D)
    convolved = depthwise(gated, taps).reshape(group_rows, D)
    local_center = jnp.mean(convolved, axis=0)
    local_offset = convolved - local_center
    moments = lax.all_gather(
        jnp.stack([local_center, jnp.sum(local_offset * local_offset, axis=0)]), "dp", axis=0
    )
    center = jnp.mean(moments[:, 0], axis=0)
    spread = moments[:, 0] - center
    variance = (jnp.sum(moments[:, 1], axis=0) + group_rows * jnp.sum(spread * spread, axis=0)) / (
        total_rows
    )
    inverse_std = lax.rsqrt(variance + epsilon)
    unit_values = (convolved - center) * inverse_std
    scaled = unit_values * affine[0] + affine[1]
    active = jax.nn.silu(scaled).astype(bfloat)
    after_three = after_two + dot("gc,dc->gd", active, w_conv)
    rows_four, norm_four = norm_input(after_three, 3)
    branch, ff_second = ff_forward(rows_four, in_one, out_one)
    after_four = after_three + 0.5 * branch
    result, norm_five = norm_rows(after_four, norm_gain[4], norm_bias[4])
    outputs = leave(result)

    counts = (me < micro).astype(single)

    def by_model(part):
        return jnp.swapaxes(part.reshape(D, mp, -1), 0, 1)

    def scatter(parts, pairs=True):
        block = jnp.concatenate([part.astype(bfloat) for part in parts], axis=2)
        if mp != micro:
            block = block * counts.astype(bfloat)
        if pairs:
            return sum_by_pairs(block).astype(single)
        return lax.psum_scatter(
            block.reshape(mp * D, -1), EVERY, scatter_dimension=0, tiled=True
        ).astype(single)

    gains = [None] * 5
    shifts = [None] * 5
    grad_four, gains[4], shifts[4] = norm_rows_back(cotangent_rows, norm_five, norm_gain[4])
    grad_rows, first_one, second_one = ff_backward(
        (0.5 * grad_four).astype(bfloat), rows_four, ff_second, in_one, out_one
    )
    owned_one = scatter([first_one, second_one], pairs=False)
    grad_norm, gains[3], shifts[3] = norm_rows_back(grad_rows, norm_four, norm_gain[3])
    grad_three = grad_four + grad_norm
    grad_out = grad_three.astype(bfloat)
    grad_conv = dot("gd,gc->dc", grad_out, active)
    grad_scaled = dot("gd,dc->gc", grad_out, w_conv) * swish_slope(scaled)
    local_shift = jnp.sum(grad_scaled, axis=0)
    local_scale = jnp.sum(grad_scaled * unit_values, axis=0)
    sums = jnp.sum(lax.all_gather(jnp.stack([local_shift, local_scale]), "dp", axis=0), axis=0)
    grad_convolved = (
        affine[0]
        * inverse_std
        * (grad_scaled - sums[0] / total_rows - unit_values * (sums[1] / total_rows))
    )
    grad_gated, grad_taps = depthwise_back(
        gated, grad_convolved.reshape(sequences, LENGTH, D), taps
    )
    grad_gated = grad_gated.reshape(group_rows, D)
    sigmoid = jax.nn.sigmoid(gate_part)
    stacked = jnp.concatenate(
        [
            (grad_gated * sigmoid).astype(bfloat),
            (grad_gated * linear_part * sigmoid * (1.0 - sigmoid)).astype(bfloat),
        ],
        axis=1,
    )
    grad_gate = dot("gd,gc->dc", rows_three, stacked)
    grad_rows = dot("gc,dc->gd", stacked, w_gate)
    grad_norm, gains[2], shifts[2] = norm_rows_back(grad_rows, norm_three, norm_gain[2])
    grad_two = grad_three + grad_norm
    grad_rows, grad_query, grad_position, grad_attn, grad_bias = attention_backward(
        grad_two.astype(bfloat), rows_two, attn_kept
    )
    owned_mats = scatter(
        [by_model(grad_query[:, k * D : (k + 1) * D]) for k in range(3)]
        + [
            by_model(part)
            for part in (grad_position, grad_gate[:, :D], grad_gate[:, D:], grad_attn, grad_conv)
        ]
    )
    grad_norm, gains[1], shifts[1] = norm_rows_back(grad_rows, norm_two, norm_gain[1])
    grad_one = grad_two + grad_norm
    grad_rows, first_zero, second_zero = ff_backward(
        (0.5 * grad_one).astype(bfloat), rows_one, ff_first, in_zero, out_zero
    )
    grad_norm, gains[0], shifts[0] = norm_rows_back(grad_rows, norm_one, norm_gain[0])
    input_grad = leave(grad_one + grad_norm)
    channel_grads = jnp.concatenate(
        [grad_taps, jnp.stack([local_scale, local_shift]), grad_bias], axis=0
    )
    channel_grads = jnp.swapaxes(channel_grads.reshape(channel_rows, owners, own), 0, 1)
    norm_grads = (
        stack_rows(gains + shifts).reshape(10, dp, mp, own).transpose(2, 1, 0, 3)
    ).reshape(owners, 10, own)
    small_grads = jnp.concatenate([channel_grads, norm_grads], axis=1).reshape(owners, -1)
    owned_zero = scatter(
        [first_zero, second_zero, fold(small_grads).reshape(mp, D, LANES)]
    )
    owned_small = owned_zero[:, 2 * hidden_width :].reshape(-1)[: (channel_rows + 10) * own]
    owned_small = owned_small.reshape(1, channel_rows + 10, own)

    def halves(owned):
        return (owned[:, :hidden_width], owned[:, hidden_width : 2 * hidden_width].T)

    first_zero, second_zero = halves(owned_zero)
    first_one, second_one = halves(owned_one)
    owned_list = [owned_mats[:, k * width : (k + 1) * width] for k in range(8)]
    return (
        outputs,
        input_grad,
        jnp.stack([first_zero, first_one])[None],
        jnp.stack([second_zero, second_one])[None],
        jnp.stack(owned_list[:6])[None],
        owned_list[6].T[None],
        owned_list[7].T[None],
        owned_small[:, :KERNEL],
        owned_small[:, KERNEL : KERNEL + 2],
        owned_small[:, KERNEL + 2 : channel_rows],
        owned_small[:, channel_rows : channel_rows + 5],
        owned_small[:, channel_rows + 5 :],
    )


def solution(mesh):
    placed = (
        P(None, ("dp", "mp"), None),
        P(None, None, "dp", "mp"),
        P(None, None, "mp", "dp"),
        P(None, None, "dp", "mp"),
        P(None, "mp", "dp"),
        P(None, "mp", "dp"),
        P(None, None, ("mp", "dp")),
        P(None, None, ("mp", "dp")),
        P(None, None, ("mp", "dp")),
        P(None, None, ("dp", "mp")),
        P(None, None, ("dp", "mp")),
        P(None, ("dp", "mp"), None),
    )
    return jax.shard_map(
        per_device,
        mesh=mesh,
        in_specs=placed,
        out_specs=(
            P(None, ("dp", "mp"), None),
            P(None, ("dp", "mp"), None),
            P(None, None, "dp", "mp"),
            P(None, None, "mp", "dp"),
            P(None, None, "dp", "mp"),
            P(None, "mp", "dp"),
            P(None, "mp", "dp"),
            P(None, None, ("mp", "dp")),
            P(None, None, ("mp", "dp")),
            P(None, None, ("mp", "dp")),
            P(None, None, ("dp", "mp")),
            P(None, None, ("dp", "mp")),
        ),
        check_vma=False,
    )
```
